256 devices in a mesh: pair: 8 (over z_hi, core), vcol: 32 (over x, y, z_lo).
Axes of the slice: x: 4, y: 4, z: 8 (z_hi: 4, z_lo: 2; z = z_hi * 2 + z_lo), core: 2. Of those that a mesh axis runs over, the one named last changes fastest.
Arguments:
- amplitudes: bfloat16 [5120, 8192], P('pair', 'vcol'), may hold values from -6 to 6
- tile_owner: int32 [64], replicated, may hold values from 0 to 63, each once
- integrals: bfloat16 [8192, 8192], P('pair', 'vcol'), may hold values from -0.125 to 0.125
- screening: int32 [80, 64, 64], P('pair'), may hold values 0 or 1
- occ_energy: float32 [5120], P('pair'), may hold values from -1 to -0.2
- virt_energy: float32 [8192], replicated, may hold values from 0.2 to 1
Outputs:
- residual: bfloat16 [5120, 8192], P('pair', 'vcol')
The draws below stay inside these ranges and needn't reach their ends.
Inputs may be any that keep to these rules, and one draw needn't show every extreme that they name: `tile_owner`: each of the 64 tiles appears exactly once.
All inputs are finite; a program needn't handle non-finite values. No bound on the sum of `screening` on one device may be relied on, other than what follows from the above.
Results may differ from the reference program's by a relative error of at most 0.0036.
Values may be sent and summed in bfloat16 or wider, within the bound.
No kernel may reach another device: no remote copies, remote signals or barrier semaphores. Data moves between devices by JAX's collectives and lax.ppermute only.
A program may use at most 64 MiB of HBM per device.

```python
import jax
import jax.numpy as jnp
from jax import lax

TILE = 128
PBLK = 64
PAIRS = 5120
KT = 64
K = 8192
NPB = 80


def plant(result, own_key, low, high):
    dims = result.shape
    index_at = [jax.random.randint(jax.random.fold_in(own_key, axis), (), 0, dims[axis]) for axis in range(len(dims))]
    result = result.at[tuple(index_at)].set(low)
    longest = dims.index(max(dims))
    index_at[longest] = (index_at[longest] + 1) % dims[longest]
    return result.at[tuple(index_at)].set(high)


def strengthened(result, own_key, source, target, shards_of, factor):
    owner, partner = [(jnp.arange(result.shape[dim]) // (result.shape[dim] // shards_of)).reshape([-1 if axis == dim else 1 for axis in range(result.ndim)]) for dim in (source, target)]
    chosen = jax.random.permutation(own_key, shards_of)[partner]
    strong = (owner == chosen) | (owner == (partner + shards_of // 2) % shards_of)
    return jnp.where(strong, factor * result, result)


def block_scale(rng, extent, pieces, smallest, top_value):
    loudness, own = 1.0, jax.random.fold_in(rng, 6)
    for dim, shards_of in pieces:
        draws = jnp.exp(jax.random.uniform(jax.random.fold_in(own, dim), (shards_of,), jnp.float32, smallest / len(pieces), top_value / len(pieces)))
        loudness = loudness * jnp.repeat(draws, extent[dim] // shards_of).reshape([-1 if axis == dim else 1 for axis in range(len(extent))])
    return loudness


def noise(stream_key, shape, scale, limit, cuts=(), kind=jnp.bfloat16):
    array = scale * jax.random.normal(stream_key, shape, jnp.float32)
    if cuts:
        array = array * block_scale(stream_key, shape, cuts, -0.22, 0.18)
    return jnp.clip(array, -limit, limit).astype(kind)


def heavy_noise(own_key, shape, deviation, reach, split, heavy, held_as=jnp.bfloat16):
    values = deviation * jax.random.normal(own_key, shape, jnp.float32)
    if split:
        values = values * block_scale(own_key, shape, split, -0.22, 0.18)
    return jnp.clip(strengthened(values, jax.random.fold_in(own_key, 3), *heavy), -reach, reach).astype(held_as)


def setup_inputs(seed: int = 0) -> dict:
    arg_keys = jax.random.split(jax.random.key(seed), 7)
    amplitudes = noise(arg_keys[0], (PAIRS, K), 1.0, 6.0, ((0, 8), (1, 32)))
    tile_owner = jax.random.permutation(arg_keys[1], KT).astype(jnp.int32)
    integrals = heavy_noise(arg_keys[2], (K, K), K ** -0.5, 0.125, ((0, 8), (1, 32)), (0, 1, 32, 2.75))
    screening = plant((jax.random.randint(arg_keys[3], (NPB, KT, KT), 0, 4) < 3).astype(jnp.int32), jax.random.fold_in(arg_keys[3], 1), 0, 1)
    occ_energy = jnp.clip(-1.0 + 0.8 * jax.random.uniform(arg_keys[4], (PAIRS,), jnp.float32) ** block_scale(arg_keys[4], (PAIRS,), ((0, 8),), -0.2, 0.2), -1.0, -0.2)
    virt_energy = jnp.clip(jax.random.uniform(arg_keys[5], (K,), jnp.float32, 0.2, 1.0), 0.2, 1.0)
    return {"amplitudes": amplitudes, "tile_owner": tile_owner, "integrals": integrals, "screening": screening, "occ_energy": occ_energy, "virt_energy": virt_energy}


def reference(amplitudes, tile_owner, integrals, screening, occ_energy, virt_energy):
    pair_count = amplitudes.shape[0]
    tile_count = tile_owner.shape[0]
    slot_tiles = amplitudes.reshape(pair_count, tile_count, TILE)
    natural = jnp.zeros_like(slot_tiles).at[:, tile_owner].set(slot_tiles).reshape(pair_count, tile_count * TILE)
    grid_ints = integrals.reshape(tile_count, TILE, tile_count, TILE)
    blocks = natural.reshape(pair_count // PBLK, PBLK, tile_count * TILE)

    def one_block(operands):
        left_rows, marks = operands
        masked = (grid_ints * marks.astype(grid_ints.dtype)[:, None, :, None]).reshape(tile_count * TILE, tile_count * TILE)
        return jnp.dot(left_rows, masked, preferred_element_type=jnp.float32)

    ladder = lax.map(one_block, (blocks, screening)).reshape(pair_count, tile_count * TILE).astype(jnp.bfloat16)
    owned_tiles = ladder.reshape(pair_count, tile_count, TILE)[:, tile_owner].reshape(pair_count, tile_count * TILE).astype(jnp.float32)
    virt_owned = virt_energy.reshape(tile_count, TILE)[tile_owner].reshape(tile_count * TILE)
    residual = owned_tiles + (virt_owned[None, :] - occ_energy[:, None]) * amplitudes.astype(jnp.float32)
    return residual.astype(jnp.bfloat16)
```

```python
import functools

import jax
import jax.numpy as jnp
from jax import lax
from jax.experimental import pallas as pl
from jax.experimental.pallas import tpu as pltpu
from jax.sharding import Mesh
from jax.sharding import PartitionSpec as P

TILE = 128
PBLK = 64
ZH, CORE, NX, NY, ZL = 4, 2, 4, 4, 2
AXES = ("zh", "core", "x", "y", "zl")


def shift(value, axis, size, by):
    return lax.ppermute(value, axis, [((i + by) % size, i) for i in range(size)])


def reorder_kernel(owner_ref, src_ref, dst_ref):
    slots = owner_ref.shape[0]
    for s in range(slots):
        t = owner_ref[s]
        src = lax.rem(t // 2, 2) * (slots // 4) + t // 4
        both = src_ref[src]
        tile = jnp.where(lax.rem(t, 2) == 0, both[:, :TILE], both[:, TILE:])
        dst_ref[s // 4, :, (s % 4) * TILE : (s % 4 + 1) * TILE] = tile


def reorder(owner, spread):
    n, rows, width = spread.shape
    return pl.pallas_call(
        reorder_kernel,
        out_shape=jax.ShapeDtypeStruct((n // 2, rows, 2 * width), spread.dtype),
        in_specs=[
            pl.BlockSpec(memory_space=pltpu.SMEM),
            pl.BlockSpec(memory_space=pltpu.VMEM),
        ],
        out_specs=pl.BlockSpec(memory_space=pltpu.VMEM),
        compiler_params=pltpu.CompilerParams(vmem_limit_bytes=8 << 20),
        cost_estimate=pl.CostEstimate(flops=0, bytes_accessed=1 << 20, transcendentals=0),
        name="reorder",
    )(owner, spread)


def line_sources():
    first, second = [], []
    for d in (0, 1, 3):
        first.append([(0, d, e) for e in range(4)])
        second.append([(1, e, d) for e in range(4)])
    first += [[(0, 2, 0), (0, 2, 1)], [(0, 2, 2), (0, 2, 3)]]
    second += [[(1, 0, 2), (1, 1, 2)], [(1, 2, 2), (1, 3, 2)]]
    return first + second


def ladder_kernel(pos_ref, owner_ref, screen_ref, panel_ref, *refs):
    sources = line_sources()
    blocks = refs[: len(sources)]
    out_ref, held, sems = refs[len(sources) :]
    x, y, zl, target = pos_ref[0], pos_ref[1], pos_ref[2], pos_ref[3]
    rows = out_ref.shape[0]
    nb = rows // PBLK
    tiles = owner_ref.shape[0]
    column = pl.multiple_of(target * 2 * TILE, 2 * TILE)
    line = (x * NY + y) * ZL + target
    wanted = [owner_ref[2 * line + i] for i in range(2)]
    pieces = [piece for block in sources for piece in block]

    def tile_of(piece, j):
        partner, dy, dx = piece
        device = (((x + dx) & 3) * NY + ((y + dy) & 3)) * ZL + (zl ^ partner)
        return owner_ref[2 * device + j]

    def copy(k, j):
        t = tile_of(pieces[k], j)
        place = ((t // 16) * 4 + lax.rem(t // 4, 2) * 2 + lax.rem(t // 8, 2)) * 4 + lax.rem(t, 4)
        return pltpu.make_async_copy(
            panel_ref.at[place, :, pl.ds(column, 2 * TILE)],
            held.at[k, pl.ds(j * TILE, TILE), :],
            sems.at[k, j],
        )

    for k in range(len(pieces)):
        for j in range(2):
            copy(k, j).start()
    totals = [None, None]
    k = 0
    for ref, block in zip(blocks, sources):
        for n in range(len(block)):
            for j in range(2):
                copy(k + n, j).wait()
        right = held[k : k + len(block)].reshape(len(block) * 2 * TILE, 2 * TILE)
        for i in range(2):
            left = []
            for n, piece in enumerate(block):
                for j in range(2):
                    t = tile_of(piece, j)
                    strips = []
                    for b in range(nb):
                        mark = screen_ref[(b * tiles + t) * tiles + wanted[i]]
                        strip = ref[n, b * PBLK : (b + 1) * PBLK, j * TILE : (j + 1) * TILE]
                        strips.append(strip * jnp.full((PBLK, TILE), mark, jnp.float32).astype(strip.dtype))
                    left.append(jnp.concatenate(strips, axis=0))
            part = jnp.dot(
                jnp.concatenate(left, axis=1),
                right[:, i * TILE : (i + 1) * TILE],
                preferred_element_type=jnp.float32,
            )
            totals[i] = part if totals[i] is None else totals[i] + part
        k += len(block)
    for i in range(2):
        out_ref[:, i * TILE : (i + 1) * TILE] = totals[i].astype(out_ref.dtype)


def ladder(pos, owner, screen, panel, blocks):
    rows, width = blocks[0].shape[1:]
    pieces = sum(b.shape[0] for b in blocks)
    smem, vmem = (pl.BlockSpec(memory_space=m) for m in (pltpu.SMEM, pltpu.VMEM))
    return pl.pallas_call(
        ladder_kernel,
        out_shape=jax.ShapeDtypeStruct((rows, width), jnp.bfloat16),
        in_specs=[smem, smem, smem, pl.BlockSpec(memory_space=pl.ANY)] + [vmem] * len(blocks),
        out_specs=vmem,
        scratch_shapes=[
            pltpu.VMEM((pieces, 2 * TILE, width), jnp.bfloat16),
            pltpu.SemaphoreType.DMA((pieces, 2)),
        ],
        compiler_params=pltpu.CompilerParams(vmem_limit_bytes=24 << 20),
        cost_estimate=pl.CostEstimate(
            flops=2 * rows * width * pieces * width,
            bytes_accessed=(rows + width) * pieces * width * 2,
            transcendentals=0,
        ),
        name="ladder",
    )(pos, owner, screen, panel, *blocks)


def gather_amplitudes(own, other):
    blocks = []
    for mine, (a, na), (b, nb) in ((own, ("x", NX), ("y", NY)), (other, ("y", NY), ("x", NX))):
        near = [shift(mine, a, na, d) for d in (1, 2, 3)]
        blocks.append(jnp.stack([mine] + near))
    for i, (b, nb) in enumerate((("y", NY), ("x", NX))):
        ahead, behind = shift(blocks[i], b, nb, 1), shift(blocks[i], b, nb, 3)
        far = [shift(ahead[:2], b, nb, 1), shift(behind[2:], b, nb, 3)]
        blocks[i] = [blocks[i], ahead, behind] + far
    return blocks[0] + blocks[1]


def local(amplitudes, tile_owner, integrals, screening, occ_energy, virt_energy):
    pairs, width = amplitudes.shape
    half = pairs // ZL
    tiles = tile_owner.shape[0]
    x, y, zl = (lax.axis_index(a) for a in ("x", "y", "zl"))
    device = (x * NY + y) * ZL + zl
    rows = integrals.shape[0] // (NX * NY * ZL)

    mine = lax.dynamic_slice_in_dim(amplitudes, zl * half, half, 0)
    other = lax.dynamic_slice_in_dim(amplitudes, (1 - zl) * half, half, 0)
    other = shift(other, "zl", ZL, 1)

    spread = lax.all_to_all(integrals.reshape(-1, rows, width), ("zl", "x", "y"), 0, 0, tiled=True)
    slots = reorder(tile_owner, spread)
    strip = lax.all_to_all(slots, ("x", "y"), 0, 0, tiled=True)
    strip, mine, other = lax.optimization_barrier((strip, mine, other))
    panel = lax.all_gather(strip.reshape(-1, ZL * width), ("zh", "zl", "core"), axis=0, tiled=True)
    panel = panel.reshape(tiles, TILE, ZL * width)
    blocks = gather_amplitudes(mine, other)

    screen = lax.dynamic_slice_in_dim(screening, zl * (half // PBLK), half // PBLK, 0)
    screen = screen.astype(jnp.float32).reshape(-1)
    place = [jnp.stack([x, y, zl, t]).astype(jnp.int32) for t in (1 - zl, zl)]
    sent = ladder(place[0], tile_owner, screen, panel, blocks)
    got = shift(sent, "zl", ZL, 1)
    kept = ladder(place[1], tile_owner, screen, panel, blocks)

    total = jnp.concatenate(
        [jnp.where(zl == 0, kept, got), jnp.where(zl == 0, got, kept)], axis=0
    ).astype(jnp.float32)
    virt_owned = jnp.concatenate(
        [
            lax.dynamic_slice_in_dim(virt_energy, tile_owner[2 * device + i] * TILE, TILE, 0)
            for i in range(2)
        ]
    )
    residual = total + (virt_owned[None, :] - occ_energy[:, None]) * amplitudes.astype(jnp.float32)
    return residual.astype(jnp.bfloat16)


def solution(mesh):
    fine = Mesh(mesh.devices.reshape(ZH, CORE, NX, NY, ZL), AXES)
    pair, vcol = ("zh", "core"), ("x", "y", "zl")
    return jax.shard_map(
        local,
        mesh=fine,
        in_specs=(P(pair, vcol), P(), P(pair, vcol), P(pair, None, None), P(pair), P()),
        out_specs=P(pair, vcol),
        check_vma=False,
    )
```

```python
import jax
import jax.numpy as jnp
from jax import lax
from jax.experimental import pallas as pl
from jax.experimental.pallas import tpu as pltpu
from jax.sharding import Mesh
from jax.sharding import PartitionSpec as P

TILE = 128
PBLK = 64
ZH, CORE, NX, NY, ZL = 4, 2, 4, 4, 2
AXES = ("zh", "core", "x", "y", "zl")
SMEM, VMEM, HBM = (
    pl.BlockSpec(memory_space=m) for m in (pltpu.SMEM, pltpu.VMEM, pltpu.HBM)
)


def shift(value, axis, size, by):
    return lax.ppermute(value, axis, [((i + by) % size, i) for i in range(size)])


def gather_amplitudes(own, other):
    blocks = []
    for mine, a, na in ((own, "x", NX), (other, "y", NY)):
        blocks.append(jnp.stack([mine] + [shift(mine, a, na, d) for d in (1, 2, 3)]))
    parts = []
    for block, b, nb in ((blocks[0], "y", NY), (blocks[1], "x", NX)):
        ahead, behind = shift(block, b, nb, 1), shift(block, b, nb, 3)
        far = [shift(ahead[:2], b, nb, 1), shift(behind[2:], b, nb, 3)]
        parts += [block, ahead, behind] + far
    order = [(0, d, e) for d in (0, 1, 3, 2) for e in range(4)]
    order += [(1, e, d) for d in (0, 1, 3, 2) for e in range(4)]
    return jnp.concatenate(parts), order


def ladder_kernel(pos_ref, place_ref, screen_ref, left_hbm, panel_ref, out_ref, left_ref, held, total, left_sem, sems):
    groups, depth, width = held.shape
    rows = left_ref.shape[1]
    tiles = place_ref.shape[0]
    line, per = pos_ref[0], depth // TILE

    def fetch(g):
        return pltpu.make_async_copy(panel_ref.at[g], held.at[g], sems.at[g])

    left_copy = pltpu.make_async_copy(left_hbm, left_ref, left_sem)
    left_copy.start()

    @pl.loop(0, groups)
    def _(g):
        fetch(g).start()

    total[...] = jnp.zeros_like(total)
    left_copy.wait()

    @pl.loop(0, groups)
    def _(g):
        fetch(g).wait()
        part = lax.rem(g // CORE, ZL)
        first = (g // (CORE * ZL) * CORE + lax.rem(g, CORE)) * per
        for j in range(width // TILE):
            wanted = (line * ZL + part) * 2 + j
            left = []
            for r in range(per):
                at = place_ref[first + r]
                column = pl.ds(pl.multiple_of(lax.rem(at, 2) * TILE, TILE), TILE)
                strips = []
                for b in range(rows // PBLK):
                    mark = screen_ref[(b * tiles + first + r) * tiles + wanted]
                    strip = left_ref[at // 2, b * PBLK : (b + 1) * PBLK, column]
                    strips.append(strip * jnp.full((PBLK, TILE), mark, jnp.float32).astype(strip.dtype))
                left.append(jnp.concatenate(strips, axis=0))
            total[part, j] += jnp.dot(
                jnp.concatenate(left, axis=1),
                held[g, :, j * TILE : (j + 1) * TILE],
                preferred_element_type=jnp.float32,
            )

    count, piece, _ = out_ref.shape
    for i in range(total.shape[0] * total.shape[1]):
        for c in range(count):
            strip = total[i // 2, i % 2, c * piece : (c + 1) * piece, :]
            out_ref[c, :, i * TILE : (i + 1) * TILE] = strip.astype(out_ref.dtype)


def ladder(pos, place, screen, left, panel):
    groups, depth, width = panel.shape
    rows = left.shape[1]
    chunks = NX * NY
    return pl.pallas_call(
        ladder_kernel,
        out_shape=jax.ShapeDtypeStruct((chunks, rows // chunks, ZL * width), jnp.bfloat16),
        in_specs=[SMEM, SMEM, SMEM, HBM, HBM],
        out_specs=VMEM,
        scratch_shapes=[
            pltpu.VMEM(left.shape, left.dtype),
            pltpu.VMEM(panel.shape, panel.dtype),
            pltpu.VMEM((ZL, width // TILE, rows, TILE), jnp.float32),
            pltpu.SemaphoreType.DMA,
            pltpu.SemaphoreType.DMA((groups,)),
        ],
        compiler_params=pltpu.CompilerParams(vmem_limit_bytes=58 << 20),
        cost_estimate=pl.CostEstimate(
            flops=2 * rows * width * groups * depth,
            bytes_accessed=(rows + width) * groups * depth * 2,
            transcendentals=0,
        ),
        name="ladder",
    )(pos, place, screen, left, panel)


def reorder_kernel(owner_ref, src_ref, dst_ref):
    for s in range(owner_ref.shape[0]):
        t = owner_ref[s]
        tile = src_ref[t // 4, :, pl.ds(pl.multiple_of(lax.rem(t, 4) * TILE, TILE), TILE)]
        device, j = s // 2, s % 2
        target = device % ZL * NX * NY + device // ZL
        dst_ref[target, :, j * TILE : (j + 1) * TILE] = tile


def reorder(owner, spread):
    n, rows, width = spread.shape
    return pl.pallas_call(
        reorder_kernel,
        out_shape=jax.ShapeDtypeStruct((n * ZL, rows, width // ZL), spread.dtype),
        in_specs=[SMEM, VMEM],
        out_specs=VMEM,
        compiler_params=pltpu.CompilerParams(vmem_limit_bytes=8 << 20),
        cost_estimate=pl.CostEstimate(flops=0, bytes_accessed=1 << 20, transcendentals=0),
        name="reorder",
    )(owner, spread)


def local(amplitudes, tile_owner, integrals, screening, occ_energy, virt_energy):
    pairs, width = amplitudes.shape
    half = pairs // ZL
    tiles = tile_owner.shape[0]
    x, y, zl = (lax.axis_index(a) for a in ("x", "y", "zl"))
    line = x * NY + y

    panel = lax.all_gather(integrals, ("zh", "zl", "core"), axis=0, tiled=False)

    mine = lax.dynamic_slice_in_dim(amplitudes, zl * half, half, 0)
    other = lax.dynamic_slice_in_dim(amplitudes, (1 - zl) * half, half, 0)
    other = shift(other, "zl", ZL, 1)
    left, order = gather_amplitudes(mine, other)

    partner, dy, dx = (jnp.array(v, jnp.int32) for v in zip(*order))
    device = (((x + dx) % NX) * NY + (y + dy) % NY) * ZL + (zl ^ partner)
    slots = (2 * device[:, None] + jnp.arange(2, dtype=jnp.int32)).reshape(-1)
    steps = jnp.arange(tiles, dtype=jnp.int32)
    held = jnp.sum(jnp.where(slots[:, None] == steps[None, :], tile_owner[None, :], 0), axis=1)
    place = jnp.sum(jnp.where(held[:, None] == steps[None, :], steps[:, None], 0), axis=0)

    screen = lax.dynamic_slice_in_dim(screening, zl * (half // PBLK), half // PBLK, 0)
    screen = screen.astype(jnp.float32).reshape(-1)
    found = ladder(jnp.stack([line]).astype(jnp.int32), place, screen, left, panel)
    spread = lax.all_to_all(found, ("x", "y"), 0, 0, tiled=True)
    sent = reorder(tile_owner, spread)
    total = lax.all_to_all(sent, ("zl", "x", "y"), 0, 0, tiled=True)
    total = total.reshape(pairs, width).astype(jnp.float32)

    own = 2 * (line * ZL + zl)
    virt_owned = jnp.concatenate(
        [lax.dynamic_slice_in_dim(virt_energy, tile_owner[own + i] * TILE, TILE, 0) for i in range(2)]
    )
    residual = total + (virt_owned[None, :] - occ_energy[:, None]) * amplitudes.astype(jnp.float32)
    return residual.astype(jnp.bfloat16)


def solution(mesh):
    fine = Mesh(mesh.devices.reshape(ZH, CORE, NX, NY, ZL), AXES)
    pair, vcol = ("zh", "core"), ("x", "y", "zl")
    return jax.shard_map(
        local,
        mesh=fine,
        in_specs=(P(pair, vcol), P(), P(pair, vcol), P(pair, None, None), P(pair), P()),
        out_specs=P(pair, vcol),
        check_vma=False,
    )
```

```python
import functools
import itertools

import jax
import jax.numpy as jnp
from jax import lax
from jax.experimental import pallas as pl
from jax.experimental.pallas import tpu as pltpu
from jax.sharding import Mesh
from jax.sharding import PartitionSpec as P

TILE = 128
PBLK = 64
ZH, CORE, NX, NY, ZL = 4, 2, 4, 4, 2
AXES = ("zh", "core", "x", "y", "zl")
SMEM, VMEM, HBM = (
    pl.BlockSpec(memory_space=m) for m in (pltpu.SMEM, pltpu.VMEM, pltpu.HBM)
)


def send(value, route):
    sizes = (ZH, CORE, NX, NY, ZL)
    pairs = []
    for at in itertools.product(*(range(n) for n in sizes)):
        source = [i % n for i, n in zip(route(*at), sizes)]
        pairs.append(tuple(functools.reduce(lambda u, v: u * v[1] + v[0], zip(p, sizes), 0) for p in (source, at)))
    return lax.ppermute(value, AXES, pairs)


def ring(value):
    def route(zh, core, x, y, zl):
        z = zh * ZL + zl + 2 * core - 1
        return z // ZL, core, x, y, z % ZL

    return send(value, route)


def swap(value):
    return send(value, lambda zh, core, x, y, zl: (zh, 1 - core, x, y, zl))


def minor(value, by):
    return send(value, lambda zh, core, x, y, zl: (zh, core, x + by * (1 - core), y + by * core, zl))


def major(value, by):
    return send(value, lambda zh, core, x, y, zl: (zh, core, x + by * core, y + by * (1 - core), zl))


def gather_amplitudes(own):
    block = jnp.stack([own] + [minor(own, d) for d in (1, 2, 3)])
    ahead, behind = major(block, 1), major(block, 3)
    far = [major(ahead[:2], 1), major(behind[2:], 3)]
    return [block, ahead, behind] + far, [(d, e) for d in (0, 1, 3, 2) for e in range(4)]


def gather_panel(own):
    near, late = [(own, (0, 0))], []
    other = swap(own)
    near.append((other, (0, 1)))
    first, second = own, other
    for d in (1, 2, 3, 4):
        out = near if d < 3 else late
        first = ring(first)
        out += [(first, (d, 0)), (swap(first), (-d, 1))]
        if d < 4:
            second = ring(second)
            out += [(second, (d, 1)), (swap(second), (-d, 0))]
    return near, late


def ladder_kernel(more, last, count, *refs):
    line_ref, first_ref, part_ref, place_ref, screen_ref = refs[:5]
    blocks, refs = refs[5:10], refs[10:]
    panels, refs = refs[:count], refs[count:]
    if more:
        before, refs = refs[0], refs[1:]
    out_ref, left_ref, held, left_sem, sems = refs[:5]
    total = refs[5] if last else out_ref
    depth, width = held.shape[1:]
    rows = left_ref.shape[1]
    tiles = place_ref.shape[0]
    line, per, wide = line_ref[0], depth // TILE, left_ref.shape[2] // TILE

    copies, at = [], 0
    for i, block in enumerate(blocks):
        n = block.shape[0]
        copies.append(pltpu.make_async_copy(block, left_ref.at[at : at + n], left_sem.at[i]))
        at += n
    fetch = [pltpu.make_async_copy(panel, held.at[g], sems.at[g]) for g, panel in enumerate(panels)]
    for c in copies + fetch:
        c.start()
    if more:
        total[...] = before[...]
    else:
        total[...] = jnp.zeros_like(total)
    for c in copies:
        c.wait()

    @pl.loop(0, count)
    def _(g):
        pltpu.make_async_copy(panels[0], held.at[g], sems.at[g]).wait()
        part, first = part_ref[g], first_ref[g]
        for j in range(width // TILE):
            wanted = (line * ZL + part) * 2 + j
            left = []
            for r in range(per):
                at = place_ref[first + r]
                column = pl.ds(pl.multiple_of(lax.rem(at, wide) * TILE, TILE), TILE)
                strips = []
                for b in range(rows // PBLK):
                    mark = screen_ref[(b * tiles + first + r) * tiles + wanted]
                    strip = left_ref[at // wide, b * PBLK : (b + 1) * PBLK, column]
                    strips.append(strip * jnp.full((PBLK, TILE), mark, jnp.float32).astype(strip.dtype))
                left.append(jnp.concatenate(strips, axis=0))
            total[part, j] += jnp.dot(
                jnp.concatenate(left, axis=1),
                held[g, :, j * TILE : (j + 1) * TILE],
                preferred_element_type=jnp.float32,
            )

    if last:
        chunks, piece, _ = out_ref.shape
        for i in range(total.shape[0] * total.shape[1]):
            for c in range(chunks):
                strip = total[i // 2, i % 2, c * piece : (c + 1) * piece, :]
                out_ref[c, :, i * TILE : (i + 1) * TILE] = strip.astype(out_ref.dtype)


def ladder(line, where, place, screen, blocks, panels, before, last):
    depth, width = panels[0].shape
    rows = blocks[0].shape[1]
    count, pieces = len(panels), sum(b.shape[0] for b in blocks)
    sums = (ZL, width // TILE, rows, TILE)
    chunks = NX * NY
    more = before is not None
    return pl.pallas_call(
        functools.partial(ladder_kernel, more, last, count),
        out_shape=jax.ShapeDtypeStruct((chunks, rows // chunks, ZL * width), jnp.bfloat16)
        if last
        else jax.ShapeDtypeStruct(sums, jnp.float32),
        in_specs=[SMEM] * 5 + [HBM] * (len(blocks) + count) + [VMEM] * more,
        out_specs=VMEM,
        scratch_shapes=[
            pltpu.VMEM((pieces,) + blocks[0].shape[1:], jnp.bfloat16),
            pltpu.VMEM((count, depth, width), jnp.bfloat16),
            pltpu.SemaphoreType.DMA((len(blocks),)),
            pltpu.SemaphoreType.DMA((count,)),
        ]
        + [pltpu.VMEM(sums, jnp.float32)] * last,
        compiler_params=pltpu.CompilerParams(vmem_limit_bytes=50 << 20),
        cost_estimate=pl.CostEstimate(
            flops=4 * rows * width * count * depth,
            bytes_accessed=(2 * rows + width) * count * depth * 2,
            transcendentals=0,
        ),
        name="ladder",
    )(line, *where, place, screen, *blocks, *panels, *([before] if more else []))


def reorder_kernel(owner_ref, src_ref, dst_ref):
    for s in range(owner_ref.shape[0]):
        t = owner_ref[s]
        tile = src_ref[t // 4, :, pl.ds(pl.multiple_of(lax.rem(t, 4) * TILE, TILE), TILE)]
        device, j = s // 2, s % 2
        target = device % ZL * NX * NY + device // ZL
        dst_ref[target, :, j * TILE : (j + 1) * TILE] = tile


def reorder(owner, spread):
    n, rows, width = spread.shape
    return pl.pallas_call(
        reorder_kernel,
        out_shape=jax.ShapeDtypeStruct((n * ZL, rows, width // ZL), spread.dtype),
        in_specs=[SMEM, VMEM],
        out_specs=VMEM,
        compiler_params=pltpu.CompilerParams(vmem_limit_bytes=8 << 20),
        cost_estimate=pl.CostEstimate(flops=0, bytes_accessed=1 << 20, transcendentals=0),
        name="reorder",
    )(owner, spread)


def local(amplitudes, tile_owner, integrals, screening, occ_energy, virt_energy):
    pairs, width = amplitudes.shape
    half = pairs // ZL
    tiles = tile_owner.shape[0]
    zh, core, x, y, zl = (lax.axis_index(a) for a in AXES)
    line = x * NY + y
    steps = jnp.arange(tiles, dtype=jnp.int32)

    mine = lax.dynamic_slice_in_dim(amplitudes, zl * half, half, 0)
    other = lax.dynamic_slice_in_dim(amplitudes, (1 - zl) * half, half, 0)
    other = send(other, lambda zh, core, x, y, zl: (zh, core, x, y, 1 - zl))
    blocks, order = gather_amplitudes(jnp.concatenate([mine, other], axis=1))
    near, late = gather_panel(integrals)

    far, close = (jnp.array(v, jnp.int32) for v in zip(*order))
    dx, dy = jnp.where(core == 0, close, far), jnp.where(core == 0, far, close)
    device = (((x + dx) % NX) * NY + (y + dy) % NY)[:, None] * ZL + (zl ^ jnp.arange(ZL, dtype=jnp.int32))
    slots = (2 * device[:, :, None] + jnp.arange(2, dtype=jnp.int32)).reshape(-1)
    held = jnp.sum(jnp.where(slots[:, None] == steps[None, :], tile_owner[None, :], 0), axis=1)
    place = jnp.sum(jnp.where(held[:, None] == steps[None, :], steps[:, None], 0), axis=0)

    screen = lax.dynamic_slice_in_dim(screening, zl * (half // PBLK), half // PBLK, 0)
    screen = screen.astype(jnp.float32).reshape(-1)
    found = None
    for last, group in ((False, near), (True, late)):
        panels, marks = zip(*group)
        step, flip = (jnp.array(v, jnp.int32) for v in zip(*marks))
        chip = (zh * ZL + zl + step * (2 * core - 1)) % (ZH * ZL)
        first = (chip // ZL * CORE + (core ^ flip)) * (integrals.shape[0] // TILE)
        where = (first.astype(jnp.int32), (chip % ZL).astype(jnp.int32))
        found = ladder(jnp.stack([line]).astype(jnp.int32), where, place, screen, blocks, panels, found, last)
    spread = lax.all_to_all(found, ("x", "y"), 0, 0, tiled=True)
    sent = reorder(tile_owner, spread)
    total = lax.all_to_all(sent, ("zl", "x", "y"), 0, 0, tiled=True)
    total = total.reshape(pairs, width).astype(jnp.float32)

    own = 2 * (line * ZL + zl)
    virt_owned = jnp.concatenate(
        [lax.dynamic_slice_in_dim(virt_energy, tile_owner[own + i] * TILE, TILE, 0) for i in range(2)]
    )
    residual = total + (virt_owned[None, :] - occ_energy[:, None]) * amplitudes.astype(jnp.float32)
    return residual.astype(jnp.bfloat16)


def solution(mesh):
    fine = Mesh(mesh.devices.reshape(ZH, CORE, NX, NY, ZL), AXES)
    pair, vcol = ("zh", "core"), ("x", "y", "zl")
    return jax.shard_map(
        local,
        mesh=fine,
        in_specs=(P(pair, vcol), P(), P(pair, vcol), P(pair, None, None), P(pair), P()),
        out_specs=P(pair, vcol),
        check_vma=False,
    )
```

```python
import functools
import itertools

import jax
import jax.numpy as jnp
from jax import lax
from jax.experimental import pallas as pl
from jax.experimental.pallas import tpu as pltpu
from jax.sharding import Mesh
from jax.sharding import PartitionSpec as P

TILE = 128
PBLK = 64
ZH, CORE, NX, NY, ZL = 4, 2, 4, 4, 2
AXES = ("zh", "core", "x", "y", "zl")
SMEM, VMEM, HBM = (
    pl.BlockSpec(memory_space=m) for m in (pltpu.SMEM, pltpu.VMEM, pltpu.HBM)
)


def send(value, route):
    sizes = (ZH, CORE, NX, NY, ZL)
    pairs = []
    for at in itertools.product(*(range(n) for n in sizes)):
        source = [i % n for i, n in zip(route(*at), sizes)]
        pairs.append(tuple(functools.reduce(lambda u, v: u * v[1] + v[0], zip(p, sizes), 0) for p in (source, at)))
    return lax.ppermute(value, AXES, pairs)


def ring(value):
    def route(zh, core, x, y, zl):
        z = zh * ZL + zl + 2 * core - 1
        return z // ZL, core, x, y, z % ZL

    return send(value, route)


def swap(value):
    return send(value, lambda zh, core, x, y, zl: (zh, 1 - core, x, y, zl))


def minor(value, by):
    return send(value, lambda zh, core, x, y, zl: (zh, core, x + by * (1 - core), y + by * core, zl))


def major(value, by):
    return send(value, lambda zh, core, x, y, zl: (zh, core, x + by * core, y + by * (1 - core), zl))


def tie(*values):
    return lax.optimization_barrier(values)


def gather(left, panel):
    other = swap(panel)
    first, second, flips = [panel], [other], []

    def advance():
        first.append(ring(first[-1]))
        flips.append(swap(first[-1]))
        if len(second) < ZH:
            second.append(ring(second[-1]))
            flips.append(swap(second[-1]))

    left, second[0] = tie(left, second[0])
    advance()
    block = jnp.stack([left] + [minor(left, d) for d in (1, 2, 3)])
    block, first[1], second[1] = tie(block, first[1], second[1])
    ahead, behind = major(block, 1), major(block, 3)
    advance()
    advance()
    ahead, behind, first[2], second[2] = tie(ahead, behind, first[2], second[2])
    far = [major(ahead[:2], 1), major(behind[2:], 3)]
    advance()
    return [block, ahead, behind] + far, first + second + flips


def amplitude_steps():
    return [(d, e) for d in (0, 1, 3, 2) for e in range(4)]


def panel_steps():
    steps = [(d, 0) for d in range(5)] + [(d, 1) for d in range(4)]
    return steps + [(-d, flip) for d in (1, 2, 3) for flip in (1, 0)] + [(-4, 1)]


def ladder_kernel(count, *refs):
    line_ref, first_ref, part_ref, place_ref, screen_ref = refs[:5]
    blocks, refs = refs[5:10], refs[10:]
    panels, refs = refs[:count], refs[count:]
    out_ref, left_ref, held, total, left_sem, sems = refs
    depth, width = held.shape[1:]
    rows = left_ref.shape[1]
    tiles = place_ref.shape[0]
    line, per, wide = line_ref[0], depth // TILE, left_ref.shape[2] // TILE

    copies, at = [], 0
    for i, block in enumerate(blocks):
        n = block.shape[0]
        copies.append(pltpu.make_async_copy(block, left_ref.at[at : at + n], left_sem.at[i]))
        at += n
    fetch = [pltpu.make_async_copy(panel, held.at[g], sems.at[g]) for g, panel in enumerate(panels)]
    for c in copies + fetch:
        c.start()
    total[...] = jnp.zeros_like(total)
    for c in copies:
        c.wait()

    @pl.loop(0, count)
    def _(g):
        pltpu.make_async_copy(panels[0], held.at[g], sems.at[g]).wait()
        part, first = part_ref[g], first_ref[g]
        for j in range(width // TILE):
            wanted = (line * ZL + part) * 2 + j
            left = []
            for r in range(per):
                at = place_ref[first + r]
                column = pl.ds(pl.multiple_of(lax.rem(at, wide) * TILE, TILE), TILE)
                strips = []
                for b in range(rows // PBLK):
                    mark = screen_ref[(b * tiles + first + r) * tiles + wanted]
                    strip = left_ref[at // wide, b * PBLK : (b + 1) * PBLK, column]
                    strips.append(strip * jnp.full((PBLK, TILE), mark, jnp.float32).astype(strip.dtype))
                left.append(jnp.concatenate(strips, axis=0))
            total[part, j] += jnp.dot(
                jnp.concatenate(left, axis=1),
                held[g, :, j * TILE : (j + 1) * TILE],
                preferred_element_type=jnp.float32,
            )

    chunks, piece, _ = out_ref.shape
    for i in range(total.shape[0] * total.shape[1]):
        for c in range(chunks):
            strip = total[i // 2, i % 2, c * piece : (c + 1) * piece, :]
            out_ref[c, :, i * TILE : (i + 1) * TILE] = strip.astype(out_ref.dtype)


def ladder(line, where, place, screen, blocks, panels):
    depth, width = panels[0].shape
    rows = blocks[0].shape[1]
    count, pieces = len(panels), sum(b.shape[0] for b in blocks)
    chunks = NX * NY
    return pl.pallas_call(
        functools.partial(ladder_kernel, count),
        out_shape=jax.ShapeDtypeStruct((chunks, rows // chunks, ZL * width), jnp.bfloat16),
        in_specs=[SMEM] * 5 + [HBM] * (len(blocks) + count),
        out_specs=VMEM,
        scratch_shapes=[
            pltpu.VMEM((pieces,) + blocks[0].shape[1:], jnp.bfloat16),
            pltpu.VMEM((count, depth, width), jnp.bfloat16),
            pltpu.VMEM((ZL, width // TILE, rows, TILE), jnp.float32),
            pltpu.SemaphoreType.DMA((len(blocks),)),
            pltpu.SemaphoreType.DMA((count,)),
        ],
        compiler_params=pltpu.CompilerParams(vmem_limit_bytes=40 << 20),
        cost_estimate=pl.CostEstimate(
            flops=2 * rows * width * count * depth,
            bytes_accessed=(rows + width) * count * depth * 2,
            transcendentals=0,
        ),
        name="ladder",
    )(line, *where, place, screen, *blocks, *panels)


def reorder_kernel(owner_ref, src_ref, dst_ref):
    for s in range(owner_ref.shape[0]):
        t = owner_ref[s]
        tile = src_ref[t // 4, :, pl.ds(pl.multiple_of(lax.rem(t, 4) * TILE, TILE), TILE)]
        device, j = s // 2, s % 2
        target = device % ZL * NX * NY + device // ZL
        dst_ref[target, :, j * TILE : (j + 1) * TILE] = tile


def reorder(owner, spread):
    n, rows, width = spread.shape
    return pl.pallas_call(
        reorder_kernel,
        out_shape=jax.ShapeDtypeStruct((n * ZL, rows, width // ZL), spread.dtype),
        in_specs=[SMEM, VMEM],
        out_specs=VMEM,
        compiler_params=pltpu.CompilerParams(vmem_limit_bytes=8 << 20),
        cost_estimate=pl.CostEstimate(flops=0, bytes_accessed=1 << 20, transcendentals=0),
        name="reorder",
    )(owner, spread)


def local(amplitudes, tile_owner, integrals, screening, occ_energy, virt_energy):
    pairs, width = amplitudes.shape
    half = pairs // ZL
    tiles = tile_owner.shape[0]
    zh, core, x, y, zl = (lax.axis_index(a) for a in AXES)
    line = x * NY + y
    steps = jnp.arange(tiles, dtype=jnp.int32)

    mine = lax.dynamic_slice_in_dim(amplitudes, zl * half, half, 0)
    other = lax.dynamic_slice_in_dim(amplitudes, (1 - zl) * half, half, 0)
    other = send(other, lambda zh, core, x, y, zl: (zh, core, x, y, 1 - zl))
    blocks, panels = gather(jnp.concatenate([mine, other], axis=1), integrals)

    far, close = (jnp.array(v, jnp.int32) for v in zip(*amplitude_steps()))
    dx, dy = jnp.where(core == 0, close, far), jnp.where(core == 0, far, close)
    device = (((x + dx) % NX) * NY + (y + dy) % NY)[:, None] * ZL + (zl ^ jnp.arange(ZL, dtype=jnp.int32))
    slots = (2 * device[:, :, None] + jnp.arange(2, dtype=jnp.int32)).reshape(-1)
    held = jnp.sum(jnp.where(slots[:, None] == steps[None, :], tile_owner[None, :], 0), axis=1)
    place = jnp.sum(jnp.where(held[:, None] == steps[None, :], steps[:, None], 0), axis=0)

    screen = lax.dynamic_slice_in_dim(screening, zl * (half // PBLK), half // PBLK, 0)
    screen = screen.astype(jnp.float32).reshape(-1)
    step, flip = (jnp.array(v, jnp.int32) for v in zip(*panel_steps()))
    chip = (zh * ZL + zl + step * (2 * core - 1)) % (ZH * ZL)
    first = (chip // ZL * CORE + (core ^ flip)) * (integrals.shape[0] // TILE)
    where = (first.astype(jnp.int32), (chip % ZL).astype(jnp.int32))
    found = ladder(jnp.stack([line]).astype(jnp.int32), where, place, screen, blocks, panels)
    spread = lax.all_to_all(found, ("x", "y"), 0, 0, tiled=True)
    sent = reorder(tile_owner, spread)
    total = lax.all_to_all(sent, ("zl", "x", "y"), 0, 0, tiled=True)
    total = total.reshape(pairs, width).astype(jnp.float32)

    own = 2 * (line * ZL + zl)
    virt_owned = jnp.concatenate(
        [lax.dynamic_slice_in_dim(virt_energy, tile_owner[own + i] * TILE, TILE, 0) for i in range(2)]
    )
    residual = total + (virt_owned[None, :] - occ_energy[:, None]) * amplitudes.astype(jnp.float32)
    return residual.astype(jnp.bfloat16)


def solution(mesh):
    fine = Mesh(mesh.devices.reshape(ZH, CORE, NX, NY, ZL), AXES)
    pair, vcol = ("zh", "core"), ("x", "y", "zl")
    return jax.shard_map(
        local,
        mesh=fine,
        in_specs=(P(pair, vcol), P(), P(pair, vcol), P(pair, None, None), P(pair), P()),
        out_specs=P(pair, vcol),
        check_vma=False,
    )
```

```python
import functools
import itertools

import jax
import jax.numpy as jnp
from jax import lax
from jax.experimental import pallas as pl
from jax.experimental.pallas import tpu as pltpu
from jax.sharding import Mesh
from jax.sharding import PartitionSpec as P

TILE = 128
PBLK = 64
ZH, CORE, NX, NY, ZL = 4, 2, 4, 4, 2
AXES = ("zh", "core", "x", "y", "zl")
SMEM, VMEM, HBM = (
    pl.BlockSpec(memory_space=m) for m in (pltpu.SMEM, pltpu.VMEM, pltpu.HBM)
)


def send(value, route):
    sizes = (ZH, CORE, NX, NY, ZL)
    pairs = []
    for at in itertools.product(*(range(n) for n in sizes)):
        source = [i % n for i, n in zip(route(*at), sizes)]
        pairs.append(tuple(functools.reduce(lambda u, v: u * v[1] + v[0], zip(p, sizes), 0) for p in (source, at)))
    return lax.ppermute(value, AXES, pairs)


def ring(value):
    def route(zh, core, x, y, zl):
        z = zh * ZL + zl + 2 * core - 1
        return z // ZL, core, x, y, z % ZL

    return send(value, route)


def swap(value):
    return send(value, lambda zh, core, x, y, zl: (zh, 1 - core, x, y, zl))


def minor(value, by):
    return send(value, lambda zh, core, x, y, zl: (zh, core, x + by * (1 - core), y + by * core, zl))


def major(value, by):
    return send(value, lambda zh, core, x, y, zl: (zh, core, x + by * core, y + by * (1 - core), zl))


def tie(*values):
    return lax.optimization_barrier(values)


def gather(left, panel):
    other = swap(panel)
    first, second, flips = [panel], [other], []

    def advance():
        first.append(ring(first[-1]))
        flips.append(swap(first[-1]))
        if len(second) < ZH:
            second.append(ring(second[-1]))
            flips.append(swap(second[-1]))

    left, second[0] = tie(left, second[0])
    next1, next3, next2 = (minor(left, d) for d in (1, 3, 2))
    advance()
    near = jnp.stack([left, next1])
    near, first[1] = tie(near, first[1])
    near_ahead = major(near, 1)
    advance()
    rest = jnp.stack([next3, next2])
    rest, first[2], second[1] = tie(rest, first[2], second[1])
    rest_behind, rest_ahead, near_behind = major(rest, 3), major(rest, 1), major(near, 3)
    advance()
    near_ahead, second[2] = tie(near_ahead, second[2])
    near_far = major(near_ahead, 1)
    rest_behind, first[3] = tie(rest_behind, first[3])
    rest_far = major(rest_behind, 3)
    advance()
    blocks = [near, rest, near_ahead, rest_ahead, near_behind, rest_behind, near_far, rest_far]
    return blocks, first + second + flips


def amplitude_steps():
    return [(d, e) for d in (0, 1, 3, 2) for e in (0, 1, 3, 2)]


def panel_steps():
    steps = [(d, 0) for d in range(5)] + [(d, 1) for d in range(4)]
    return steps + [(-d, flip) for d in (1, 2, 3) for flip in (1, 0)] + [(-4, 1)]


def ladder_kernel(count, *refs):
    line_ref, first_ref, part_ref, place_ref, screen_ref = refs[:5]
    blocks, refs = refs[5:13], refs[13:]
    panels, refs = refs[:count], refs[count:]
    out_ref, left_ref, held, total, left_sem, sems = refs
    depth, width = held.shape[1:]
    rows = left_ref.shape[1]
    tiles = place_ref.shape[0]
    line, per, wide = line_ref[0], depth // TILE, left_ref.shape[2] // TILE

    copies, at = [], 0
    for i, block in enumerate(blocks):
        n = block.shape[0]
        copies.append(pltpu.make_async_copy(block, left_ref.at[at : at + n], left_sem.at[i]))
        at += n
    fetch = [pltpu.make_async_copy(panel, held.at[g], sems.at[g]) for g, panel in enumerate(panels)]
    for c in copies + fetch:
        c.start()
    total[...] = jnp.zeros_like(total)
    for c in copies:
        c.wait()

    @pl.loop(0, count)
    def _(g):
        pltpu.make_async_copy(panels[0], held.at[g], sems.at[g]).wait()
        part, first = part_ref[g], first_ref[g]
        for j in range(width // TILE):
            wanted = (line * ZL + part) * 2 + j
            left = []
            for r in range(per):
                at = place_ref[first + r]
                column = pl.ds(pl.multiple_of(lax.rem(at, wide) * TILE, TILE), TILE)
                strips = []
                for b in range(rows // PBLK):
                    mark = screen_ref[(b * tiles + first + r) * tiles + wanted]
                    strip = left_ref[at // wide, b * PBLK : (b + 1) * PBLK, column]
                    strips.append(strip * jnp.full((PBLK, TILE), mark, jnp.float32).astype(strip.dtype))
                left.append(jnp.concatenate(strips, axis=0))
            total[part, j] += jnp.dot(
                jnp.concatenate(left, axis=1),
                held[g, :, j * TILE : (j + 1) * TILE],
                preferred_element_type=jnp.float32,
            )

    chunks, piece, _ = out_ref.shape
    for i in range(total.shape[0] * total.shape[1]):
        for c in range(chunks):
            strip = total[i // 2, i % 2, c * piece : (c + 1) * piece, :]
            out_ref[c, :, i * TILE : (i + 1) * TILE] = strip.astype(out_ref.dtype)


def ladder(line, where, place, screen, blocks, panels):
    depth, width = panels[0].shape
    rows = blocks[0].shape[1]
    count, pieces = len(panels), sum(b.shape[0] for b in blocks)
    chunks = NX * NY
    return pl.pallas_call(
        functools.partial(ladder_kernel, count),
        out_shape=jax.ShapeDtypeStruct((chunks, rows // chunks, ZL * width), jnp.bfloat16),
        in_specs=[SMEM] * 5 + [HBM] * (len(blocks) + count),
        out_specs=VMEM,
        scratch_shapes=[
            pltpu.VMEM((pieces,) + blocks[0].shape[1:], jnp.bfloat16),
            pltpu.VMEM((count, depth, width), jnp.bfloat16),
            pltpu.VMEM((ZL, width // TILE, rows, TILE), jnp.float32),
            pltpu.SemaphoreType.DMA((len(blocks),)),
            pltpu.SemaphoreType.DMA((count,)),
        ],
        compiler_params=pltpu.CompilerParams(vmem_limit_bytes=40 << 20),
        cost_estimate=pl.CostEstimate(
            flops=2 * rows * width * count * depth,
            bytes_accessed=(rows + width) * count * depth * 2,
            transcendentals=0,
        ),
        name="ladder",
    )(line, *where, place, screen, *blocks, *panels)


def reorder_kernel(owner_ref, src_ref, dst_ref):
    for s in range(owner_ref.shape[0]):
        t = owner_ref[s]
        tile = src_ref[t // 4, :, pl.ds(pl.multiple_of(lax.rem(t, 4) * TILE, TILE), TILE)]
        device, j = s // 2, s % 2
        target = device % ZL * NX * NY + device // ZL
        dst_ref[target, :, j * TILE : (j + 1) * TILE] = tile


def reorder(owner, spread):
    n, rows, width = spread.shape
    return pl.pallas_call(
        reorder_kernel,
        out_shape=jax.ShapeDtypeStruct((n * ZL, rows, width // ZL), spread.dtype),
        in_specs=[SMEM, VMEM],
        out_specs=VMEM,
        compiler_params=pltpu.CompilerParams(vmem_limit_bytes=8 << 20),
        cost_estimate=pl.CostEstimate(flops=0, bytes_accessed=1 << 20, transcendentals=0),
        name="reorder",
    )(owner, spread)


def local(amplitudes, tile_owner, integrals, screening, occ_energy, virt_energy):
    pairs, width = amplitudes.shape
    half = pairs // ZL
    tiles = tile_owner.shape[0]
    zh, core, x, y, zl = (lax.axis_index(a) for a in AXES)
    line = x * NY + y
    steps = jnp.arange(tiles, dtype=jnp.int32)

    mine = lax.dynamic_slice_in_dim(amplitudes, zl * half, half, 0)
    other = lax.dynamic_slice_in_dim(amplitudes, (1 - zl) * half, half, 0)
    other = send(other, lambda zh, core, x, y, zl: (zh, core, x, y, 1 - zl))
    blocks, panels = gather(jnp.concatenate([mine, other], axis=1), integrals)

    far, close = (jnp.array(v, jnp.int32) for v in zip(*amplitude_steps()))
    dx, dy = jnp.where(core == 0, close, far), jnp.where(core == 0, far, close)
    device = (((x + dx) % NX) * NY + (y + dy) % NY)[:, None] * ZL + (zl ^ jnp.arange(ZL, dtype=jnp.int32))
    slots = (2 * device[:, :, None] + jnp.arange(2, dtype=jnp.int32)).reshape(-1)
    held = jnp.sum(jnp.where(slots[:, None] == steps[None, :], tile_owner[None, :], 0), axis=1)
    place = jnp.sum(jnp.where(held[:, None] == steps[None, :], steps[:, None], 0), axis=0)

    screen = lax.dynamic_slice_in_dim(screening, zl * (half // PBLK), half // PBLK, 0)
    screen = screen.astype(jnp.float32).reshape(-1)
    step, flip = (jnp.array(v, jnp.int32) for v in zip(*panel_steps()))
    chip = (zh * ZL + zl + step * (2 * core - 1)) % (ZH * ZL)
    first = (chip // ZL * CORE + (core ^ flip)) * (integrals.shape[0] // TILE)
    where = (first.astype(jnp.int32), (chip % ZL).astype(jnp.int32))
    found = ladder(jnp.stack([line]).astype(jnp.int32), where, place, screen, blocks, panels)
    spread = lax.all_to_all(found, ("x", "y"), 0, 0, tiled=True)
    sent = reorder(tile_owner, spread)
    total = lax.all_to_all(sent, ("zl", "x", "y"), 0, 0, tiled=True)
    total = total.reshape(pairs, width).astype(jnp.float32)

    own = 2 * (line * ZL + zl)
    virt_owned = jnp.concatenate(
        [lax.dynamic_slice_in_dim(virt_energy, tile_owner[own + i] * TILE, TILE, 0) for i in range(2)]
    )
    residual = total + (virt_owned[None, :] - occ_energy[:, None]) * amplitudes.astype(jnp.float32)
    return residual.astype(jnp.bfloat16)


def solution(mesh):
    fine = Mesh(mesh.devices.reshape(ZH, CORE, NX, NY, ZL), AXES)
    pair, vcol = ("zh", "core"), ("x", "y", "zl")
    return jax.shard_map(
        local,
        mesh=fine,
        in_specs=(P(pair, vcol), P(), P(pair, vcol), P(pair, None, None), P(pair), P()),
        out_specs=P(pair, vcol),
        check_vma=False,
    )
```

```python
import functools
import itertools

import jax
import jax.numpy as jnp
from jax import lax
from jax.experimental import pallas as pl
from jax.experimental.pallas import tpu as pltpu
from jax.sharding import Mesh
from jax.sharding import PartitionSpec as P

TILE = 128
PBLK = 64
ZH, CORE, NX, NY, ZL = 4, 2, 4, 4, 2
AXES = ("zh", "core", "x", "y", "zl")
SMEM, VMEM, HBM = (
    pl.BlockSpec(memory_space=m) for m in (pltpu.SMEM, pltpu.VMEM, pltpu.HBM)
)


def send(value, route):
    sizes = (ZH, CORE, NX, NY, ZL)
    pairs = []
    for at in itertools.product(*(range(n) for n in sizes)):
        source = [i % n for i, n in zip(route(*at), sizes)]
        pairs.append(tuple(functools.reduce(lambda u, v: u * v[1] + v[0], zip(p, sizes), 0) for p in (source, at)))
    return lax.ppermute(value, AXES, pairs)


def ring(value):
    def route(zh, core, x, y, zl):
        z = zh * ZL + zl + 2 * core - 1
        return z // ZL, core, x, y, z % ZL

    return send(value, route)


def swap(value):
    return send(value, lambda zh, core, x, y, zl: (zh, 1 - core, x, y, zl))


def minor(value, by):
    return send(value, lambda zh, core, x, y, zl: (zh, core, x + by * (1 - core), y + by * core, zl))


def major(value, by):
    return send(value, lambda zh, core, x, y, zl: (zh, core, x + by * core, y + by * (1 - core), zl))


def tie(*values):
    return lax.optimization_barrier(values)


def gather(left, panel):
    other = swap(panel)
    left, other = tie(left, other)
    first, second, flips = [panel], [other], []

    def advance():
        first.append(ring(first[-1]))
        if len(second) < ZH:
            second.append(ring(second[-1]))

    advance()
    nearest = minor(left, 1)
    first[1], nearest = tie(first[1], nearest)
    block = jnp.stack([left, nearest] + [minor(left, d) for d in (2, 3)])
    advance()
    block, first[2], second[1] = tie(block, first[2], second[1])
    ahead, behind = major(block, 1), major(block, 3)
    advance()
    advance()
    ahead, first[3], second[3] = tie(ahead, first[3], second[3])
    behind, first[4] = tie(behind, first[4])
    far = [major(ahead[:2], 1), major(behind[2:], 3)]
    both = [jnp.stack([a, b]) for a, b in zip(first[1:], second[1:])]
    flips = [swap(b) for b in both] + [swap(first[-1])]
    return [block, ahead, behind] + far, [panel, other] + both + flips[:-1] + [first[-1], flips[-1]]


def amplitude_steps():
    return [(d, e) for d in (0, 1, 3, 2) for e in range(4)]


def panel_steps():
    steps = [(0, 0), (0, 1)] + [(d, flip) for d in (1, 2, 3) for flip in (0, 1)]
    return steps + [(-d, flip) for d in (1, 2, 3) for flip in (1, 0)] + [(4, 0), (-4, 1)]


def ladder_kernel(count, *refs):
    line_ref, first_ref, part_ref, place_ref, screen_ref = refs[:5]
    blocks, refs = refs[5:10], refs[10:]
    panels, refs = refs[:count], refs[count:]
    out_ref, left_ref, held, total, left_sem, sems = refs
    depth, width = held.shape[1:]
    rows = left_ref.shape[1]
    tiles = place_ref.shape[0]
    line, per, wide = line_ref[0], depth // TILE, left_ref.shape[2] // TILE

    copies, at = [], 0
    for i, block in enumerate(blocks):
        n = block.shape[0]
        copies.append(pltpu.make_async_copy(block, left_ref.at[at : at + n], left_sem.at[i]))
        at += n
    fetch, g = [], 0
    for panel in panels:
        for part in [panel] if len(panel.shape) == 2 else [panel.at[i] for i in range(panel.shape[0])]:
            fetch.append(pltpu.make_async_copy(part, held.at[g], sems.at[g]))
            g += 1
    for c in copies + fetch:
        c.start()
    total[...] = jnp.zeros_like(total)
    for c in copies:
        c.wait()

    @pl.loop(0, held.shape[0])
    def _(g):
        pltpu.make_async_copy(panels[0], held.at[g], sems.at[g]).wait()
        part, first = part_ref[g], first_ref[g]
        for j in range(width // TILE):
            wanted = (line * ZL + part) * 2 + j
            left = []
            for r in range(per):
                at = place_ref[first + r]
                column = pl.ds(pl.multiple_of(lax.rem(at, wide) * TILE, TILE), TILE)
                strips = []
                for b in range(rows // PBLK):
                    mark = screen_ref[(b * tiles + first + r) * tiles + wanted]
                    strip = left_ref[at // wide, b * PBLK : (b + 1) * PBLK, column]
                    strips.append(strip * jnp.full((PBLK, TILE), mark, jnp.float32).astype(strip.dtype))
                left.append(jnp.concatenate(strips, axis=0))
            total[part, j] += jnp.dot(
                jnp.concatenate(left, axis=1),
                held[g, :, j * TILE : (j + 1) * TILE],
                preferred_element_type=jnp.float32,
            )

    chunks, piece, _ = out_ref.shape
    for i in range(total.shape[0] * total.shape[1]):
        for c in range(chunks):
            strip = total[i // 2, i % 2, c * piece : (c + 1) * piece, :]
            out_ref[c, :, i * TILE : (i + 1) * TILE] = strip.astype(out_ref.dtype)


def ladder(line, where, place, screen, blocks, panels):
    depth, width = panels[0].shape
    rows = blocks[0].shape[1]
    count, pieces = where[0].shape[0], sum(b.shape[0] for b in blocks)
    chunks = NX * NY
    return pl.pallas_call(
        functools.partial(ladder_kernel, len(panels)),
        out_shape=jax.ShapeDtypeStruct((chunks, rows // chunks, ZL * width), jnp.bfloat16),
        in_specs=[SMEM] * 5 + [HBM] * (len(blocks) + len(panels)),
        out_specs=VMEM,
        scratch_shapes=[
            pltpu.VMEM((pieces,) + blocks[0].shape[1:], jnp.bfloat16),
            pltpu.VMEM((count, depth, width), jnp.bfloat16),
            pltpu.VMEM((ZL, width // TILE, rows, TILE), jnp.float32),
            pltpu.SemaphoreType.DMA((len(blocks),)),
            pltpu.SemaphoreType.DMA((count,)),
        ],
        compiler_params=pltpu.CompilerParams(vmem_limit_bytes=40 << 20),
        cost_estimate=pl.CostEstimate(
            flops=2 * rows * width * count * depth,
            bytes_accessed=(rows + width) * count * depth * 2,
            transcendentals=0,
        ),
        name="ladder",
    )(line, *where, place, screen, *blocks, *panels)


def reorder_kernel(owner_ref, src_ref, dst_ref):
    for s in range(owner_ref.shape[0]):
        t = owner_ref[s]
        tile = src_ref[t // 4, :, pl.ds(pl.multiple_of(lax.rem(t, 4) * TILE, TILE), TILE)]
        device, j = s // 2, s % 2
        target = device % ZL * NX * NY + device // ZL
        dst_ref[target, :, j * TILE : (j + 1) * TILE] = tile


def reorder(owner, spread):
    n, rows, width = spread.shape
    return pl.pallas_call(
        reorder_kernel,
        out_shape=jax.ShapeDtypeStruct((n * ZL, rows, width // ZL), spread.dtype),
        in_specs=[SMEM, VMEM],
        out_specs=VMEM,
        compiler_params=pltpu.CompilerParams(vmem_limit_bytes=8 << 20),
        cost_estimate=pl.CostEstimate(flops=0, bytes_accessed=1 << 20, transcendentals=0),
        name="reorder",
    )(owner, spread)


def local(amplitudes, tile_owner, integrals, screening, occ_energy, virt_energy):
    pairs, width = amplitudes.shape
    half = pairs // ZL
    tiles = tile_owner.shape[0]
    zh, core, x, y, zl = (lax.axis_index(a) for a in AXES)
    line = x * NY + y
    steps = jnp.arange(tiles, dtype=jnp.int32)

    mine = lax.dynamic_slice_in_dim(amplitudes, zl * half, half, 0)
    other = lax.dynamic_slice_in_dim(amplitudes, (1 - zl) * half, half, 0)
    other = send(other, lambda zh, core, x, y, zl: (zh, core, x, y, 1 - zl))
    blocks, panels = gather(jnp.concatenate([mine, other], axis=1), integrals)

    far, close = (jnp.array(v, jnp.int32) for v in zip(*amplitude_steps()))
    dx, dy = jnp.where(core == 0, close, far), jnp.where(core == 0, far, close)
    device = (((x + dx) % NX) * NY + (y + dy) % NY)[:, None] * ZL + (zl ^ jnp.arange(ZL, dtype=jnp.int32))
    slots = (2 * device[:, :, None] + jnp.arange(2, dtype=jnp.int32)).reshape(-1)
    held = jnp.sum(jnp.where(slots[:, None] == steps[None, :], tile_owner[None, :], 0), axis=1)
    place = jnp.sum(jnp.where(held[:, None] == steps[None, :], steps[:, None], 0), axis=0)

    screen = lax.dynamic_slice_in_dim(screening, zl * (half // PBLK), half // PBLK, 0)
    screen = screen.astype(jnp.float32).reshape(-1)
    step, flip = (jnp.array(v, jnp.int32) for v in zip(*panel_steps()))
    chip = (zh * ZL + zl + step * (2 * core - 1)) % (ZH * ZL)
    first = (chip // ZL * CORE + (core ^ flip)) * (integrals.shape[0] // TILE)
    where = (first.astype(jnp.int32), (chip % ZL).astype(jnp.int32))
    found = ladder(jnp.stack([line]).astype(jnp.int32), where, place, screen, blocks, panels)
    spread = lax.all_to_all(found, ("x", "y"), 0, 0, tiled=True)
    sent = reorder(tile_owner, spread)
    total = lax.all_to_all(sent, ("zl", "x", "y"), 0, 0, tiled=True)
    total = total.reshape(pairs, width).astype(jnp.float32)

    own = 2 * (line * ZL + zl)
    virt_owned = jnp.concatenate(
        [lax.dynamic_slice_in_dim(virt_energy, tile_owner[own + i] * TILE, TILE, 0) for i in range(2)]
    )
    residual = total + (virt_owned[None, :] - occ_energy[:, None]) * amplitudes.astype(jnp.float32)
    return residual.astype(jnp.bfloat16)


def solution(mesh):
    fine = Mesh(mesh.devices.reshape(ZH, CORE, NX, NY, ZL), AXES)
    pair, vcol = ("zh", "core"), ("x", "y", "zl")
    return jax.shard_map(
        local,
        mesh=fine,
        in_specs=(P(pair, vcol), P(), P(pair, vcol), P(pair, None, None), P(pair), P()),
        out_specs=P(pair, vcol),
        check_vma=False,
    )
```

```python
import functools
import itertools

import jax
import jax.numpy as jnp
from jax import lax
from jax.experimental import pallas as pl
from jax.experimental.pallas import tpu as pltpu
from jax.sharding import Mesh
from jax.sharding import PartitionSpec as P

TILE = 128
PBLK = 64
ZH, CORE, NX, NY, ZL = 4, 2, 4, 4, 2
AXES = ("zh", "core", "x", "y", "zl")
SMEM, VMEM, HBM = (
    pl.BlockSpec(memory_space=m) for m in (pltpu.SMEM, pltpu.VMEM, pltpu.HBM)
)


def send(value, route):
    sizes = (ZH, CORE, NX, NY, ZL)
    pairs = []
    for at in itertools.product(*(range(n) for n in sizes)):
        source = [i % n for i, n in zip(route(*at), sizes)]
        pairs.append(tuple(functools.reduce(lambda u, v: u * v[1] + v[0], zip(p, sizes), 0) for p in (source, at)))
    return lax.ppermute(value, AXES, pairs)


def ring(value):
    def route(zh, core, x, y, zl):
        z = zh * ZL + zl + 2 * core - 1
        return z // ZL, core, x, y, z % ZL

    return send(value, route)


def swap(value):
    return send(value, lambda zh, core, x, y, zl: (zh, 1 - core, x, y, zl))


def minor(value, by):
    return send(value, lambda zh, core, x, y, zl: (zh, core, x + by * (1 - core), y + by * core, zl))


def major(value, by):
    return send(value, lambda zh, core, x, y, zl: (zh, core, x + by * core, y + by * (1 - core), zl))


def tie(*values):
    return lax.optimization_barrier(values)


def gather(left, panel):
    other = swap(panel)
    first, second, flips = [panel], [other], []

    def advance():
        first.append(ring(first[-1]))
        flips.append(swap(first[-1]))
        if len(second) < ZH:
            second.append(ring(second[-1]))
            flips.append(swap(second[-1]))

    left, second[0] = tie(left, second[0])
    advance()
    block = jnp.stack([left] + [minor(left, d) for d in (1, 2, 3)])
    block, first[1], second[1] = tie(block, first[1], second[1])
    ahead, behind = major(block, 1), major(block, 3)
    advance()
    advance()
    ahead, behind, first[2], second[2] = tie(ahead, behind, first[2], second[2])
    far = [major(ahead[:2], 1), major(behind[2:], 3)]
    advance()
    return [block, ahead, behind] + far, first + second + flips


def amplitude_steps():
    return [(d, e) for d in (0, 1, 3, 2) for e in range(4)]


def panel_steps():
    steps = [(d, 0) for d in range(5)] + [(d, 1) for d in range(4)]
    return steps + [(-d, flip) for d in (1, 2, 3) for flip in (1, 0)] + [(-4, 1)]


def ladder_kernel(count, *refs):
    first_ref, part_ref, place_ref, screen_ref = refs[:4]
    blocks, refs = refs[4:9], refs[9:]
    panels, refs = refs[:count], refs[count:]
    out_ref, left_ref, held, total, left_sem, sems = refs
    depth, width = held.shape[1:]
    rows = left_ref.shape[1]
    tiles = place_ref.shape[0]
    per, wide, across = depth // TILE, left_ref.shape[2] // TILE, ZL * width // TILE

    copies, at = [], 0
    for i, block in enumerate(blocks):
        n = block.shape[0]
        copies.append(pltpu.make_async_copy(block, left_ref.at[at : at + n], left_sem.at[i]))
        at += n
    fetch = [pltpu.make_async_copy(panel, held.at[g], sems.at[g]) for g, panel in enumerate(panels)]
    for c in copies + fetch:
        c.start()
    total[...] = jnp.zeros_like(total)
    for c in copies:
        c.wait()

    @pl.loop(0, count)
    def _(g):
        pltpu.make_async_copy(panels[0], held.at[g], sems.at[g]).wait()
        part, first = part_ref[g], first_ref[g]
        for j in range(width // TILE):
            left = []
            for r in range(per):
                at = place_ref[first + r]
                column = pl.ds(pl.multiple_of(lax.rem(at, wide) * TILE, TILE), TILE)
                strips = []
                for b in range(rows // PBLK):
                    mark = screen_ref[(b * tiles + first + r) * across + part * (width // TILE) + j]
                    strip = left_ref[at // wide, b * PBLK : (b + 1) * PBLK, column]
                    strips.append(strip * jnp.full((PBLK, TILE), mark, jnp.float32).astype(strip.dtype))
                left.append(jnp.concatenate(strips, axis=0))
            total[part, j] += jnp.dot(
                jnp.concatenate(left, axis=1),
                held[g, :, j * TILE : (j + 1) * TILE],
                preferred_element_type=jnp.float32,
            )

    chunks, piece, _ = out_ref.shape
    for i in range(total.shape[0] * total.shape[1]):
        for c in range(chunks):
            strip = total[i // 2, i % 2, c * piece : (c + 1) * piece, :]
            out_ref[c, :, i * TILE : (i + 1) * TILE] = strip.astype(out_ref.dtype)


def ladder(where, place, screen, blocks, panels):
    depth, width = panels[0].shape
    rows = blocks[0].shape[1]
    count, pieces = len(panels), sum(b.shape[0] for b in blocks)
    chunks = NX * NY
    return pl.pallas_call(
        functools.partial(ladder_kernel, count),
        out_shape=jax.ShapeDtypeStruct((chunks, rows // chunks, ZL * width), jnp.bfloat16),
        in_specs=[SMEM] * 4 + [HBM] * (len(blocks) + count),
        out_specs=VMEM,
        scratch_shapes=[
            pltpu.VMEM((pieces,) + blocks[0].shape[1:], jnp.bfloat16),
            pltpu.VMEM((count, depth, width), jnp.bfloat16),
            pltpu.VMEM((ZL, width // TILE, rows, TILE), jnp.float32),
            pltpu.SemaphoreType.DMA((len(blocks),)),
            pltpu.SemaphoreType.DMA((count,)),
        ],
        compiler_params=pltpu.CompilerParams(vmem_limit_bytes=40 << 20),
        cost_estimate=pl.CostEstimate(
            flops=2 * rows * width * count * depth,
            bytes_accessed=(rows + width) * count * depth * 2,
            transcendentals=0,
        ),
        name="ladder",
    )(*where, place, screen, *blocks, *panels)


def reorder_kernel(owner_ref, src_ref, dst_ref):
    for s in range(owner_ref.shape[0]):
        t = owner_ref[s]
        tile = src_ref[t // 4, :, pl.ds(pl.multiple_of(lax.rem(t, 4) * TILE, TILE), TILE)]
        device, j = s // 2, s % 2
        target = device % ZL * NX * NY + device // ZL
        dst_ref[target, :, j * TILE : (j + 1) * TILE] = tile


def reorder(owner, spread):
    n, rows, width = spread.shape
    return pl.pallas_call(
        reorder_kernel,
        out_shape=jax.ShapeDtypeStruct((n * ZL, rows, width // ZL), spread.dtype),
        in_specs=[SMEM, VMEM],
        out_specs=VMEM,
        compiler_params=pltpu.CompilerParams(vmem_limit_bytes=8 << 20),
        cost_estimate=pl.CostEstimate(flops=0, bytes_accessed=1 << 20, transcendentals=0),
        name="reorder",
    )(owner, spread)


def local(amplitudes, tile_owner, integrals, screening, occ_energy, virt_energy):
    pairs, width = amplitudes.shape
    half = pairs // ZL
    tiles = tile_owner.shape[0]
    zh, core, x, y, zl = (lax.axis_index(a) for a in AXES)
    line = x * NY + y
    steps = jnp.arange(tiles, dtype=jnp.int32)

    other = lax.dynamic_slice_in_dim(amplitudes, (1 - zl) * half, half, 0)
    other = send(other, lambda zh, core, x, y, zl: (zh, core, x, y, 1 - zl))
    mine = lax.dynamic_slice_in_dim(amplitudes, zl * half, half, 0)
    blocks, panels = gather(jnp.concatenate([mine, other], axis=1), integrals)

    far, close = (jnp.array(v, jnp.int32) for v in zip(*amplitude_steps()))
    dx, dy = jnp.where(core == 0, close, far), jnp.where(core == 0, far, close)
    device = (((x + dx) % NX) * NY + (y + dy) % NY)[:, None] * ZL + (zl ^ jnp.arange(ZL, dtype=jnp.int32))
    slots = (2 * device[:, :, None] + jnp.arange(2, dtype=jnp.int32)).reshape(-1)
    held = jnp.sum(jnp.where(slots[:, None] == steps[None, :], tile_owner[None, :], 0), axis=1)
    place = jnp.sum(jnp.where(held[:, None] == steps[None, :], steps[:, None], 0), axis=0)

    across = ZL * width // TILE
    screen = lax.dynamic_slice(
        screening, (zl * (half // PBLK), 0, line * across), (half // PBLK, tiles, across)
    )
    screen = screen.astype(jnp.float32).reshape(-1)
    step, flip = (jnp.array(v, jnp.int32) for v in zip(*panel_steps()))
    chip = (zh * ZL + zl + step * (2 * core - 1)) % (ZH * ZL)
    first = (chip // ZL * CORE + (core ^ flip)) * (integrals.shape[0] // TILE)
    where = (first.astype(jnp.int32), (chip % ZL).astype(jnp.int32))
    found = ladder(where, place, screen, blocks, panels)
    spread = lax.all_to_all(found, ("x", "y"), 0, 0, tiled=True)
    sent = reorder(tile_owner, spread)
    total = lax.all_to_all(sent, ("zl", "x", "y"), 0, 0, tiled=True)
    total = total.reshape(pairs, width).astype(jnp.float32)

    own = 2 * (line * ZL + zl)
    virt_owned = jnp.concatenate(
        [lax.dynamic_slice_in_dim(virt_energy, tile_owner[own + i] * TILE, TILE, 0) for i in range(2)]
    )
    residual = total + (virt_owned[None, :] - occ_energy[:, None]) * amplitudes.astype(jnp.float32)
    return residual.astype(jnp.bfloat16)


def solution(mesh):
    fine = Mesh(mesh.devices.reshape(ZH, CORE, NX, NY, ZL), AXES)
    pair, vcol = ("zh", "core"), ("x", "y", "zl")
    return jax.shard_map(
        local,
        mesh=fine,
        in_specs=(P(pair, vcol), P(), P(pair, vcol), P(pair, None, None), P(pair), P()),
        out_specs=P(pair, vcol),
        check_vma=False,
    )
```

```python
import functools
import itertools

import jax
import jax.numpy as jnp
from jax import lax
from jax.experimental import pallas as pl
from jax.experimental.pallas import tpu as pltpu
from jax.sharding import Mesh
from jax.sharding import PartitionSpec as P

TILE = 128
PBLK = 64
ZH, CORE, NX, NY, ZL = 4, 2, 4, 4, 2
AXES = ("zh", "core", "x", "y", "zl")
SMEM, VMEM, HBM = (
    pl.BlockSpec(memory_space=m) for m in (pltpu.SMEM, pltpu.VMEM, pltpu.HBM)
)


def send(value, route):
    sizes = (ZH, CORE, NX, NY, ZL)
    pairs = []
    for at in itertools.product(*(range(n) for n in sizes)):
        source = [i % n for i, n in zip(route(*at), sizes)]
        pairs.append(tuple(functools.reduce(lambda u, v: u * v[1] + v[0], zip(p, sizes), 0) for p in (source, at)))
    return lax.ppermute(value, AXES, pairs)


def ring(value):
    def route(zh, core, x, y, zl):
        z = zh * ZL + zl + 2 * core - 1
        return z // ZL, core, x, y, z % ZL

    return send(value, route)


def swap(value):
    return send(value, lambda zh, core, x, y, zl: (zh, 1 - core, x, y, zl))


def minor(value, by):
    return send(value, lambda zh, core, x, y, zl: (zh, core, x + by * (1 - core), y + by * core, zl))


def major(value, by):
    return send(value, lambda zh, core, x, y, zl: (zh, core, x + by * core, y + by * (1 - core), zl))


def tie(*values):
    return lax.optimization_barrier(values)


def gather(left, panel):
    other = swap(panel)
    first, second, flips = [panel], [other], []

    def advance():
        first.append(ring(first[-1]))
        flips.append(swap(first[-1]))
        if len(second) < ZH:
            second.append(ring(second[-1]))
            flips.append(swap(second[-1]))

    left, second[0] = tie(left, second[0])
    advance()
    block = jnp.stack([left] + [minor(left, d) for d in (1, 2, 3)])
    block, first[1], second[1] = tie(block, first[1], second[1])
    ahead, behind = major(block, 1), major(block, 3)
    advance()
    advance()
    ahead, first[2], second[2] = tie(ahead, first[2], second[2])
    far = [major(ahead[:2], 1), major(behind[2:], 3)]
    advance()
    return [block, ahead, behind] + far, first + second + flips


def amplitude_steps():
    return [(d, e) for d in (0, 1, 3, 2) for e in range(4)]


def panel_steps():
    steps = [(d, 0) for d in range(5)] + [(d, 1) for d in range(4)]
    return steps + [(-d, flip) for d in (1, 2, 3) for flip in (1, 0)] + [(-4, 1)]


def ladder_kernel(count, *refs):
    first_ref, part_ref, place_ref, screen_ref = refs[:4]
    blocks, refs = refs[4:9], refs[9:]
    panels, refs = refs[:count], refs[count:]
    out_ref, left_ref, held, total, left_sem, sems = refs
    depth, width = held.shape[1:]
    rows = left_ref.shape[1]
    tiles = place_ref.shape[0]
    per, wide, across = depth // TILE, left_ref.shape[2] // TILE, ZL * width // TILE

    copies, at = [], 0
    for i, block in enumerate(blocks):
        n = block.shape[0]
        copies.append(pltpu.make_async_copy(block, left_ref.at[at : at + n], left_sem.at[i]))
        at += n
    fetch = [pltpu.make_async_copy(panel, held.at[g], sems.at[g]) for g, panel in enumerate(panels)]
    for c in copies + fetch:
        c.start()
    total[...] = jnp.zeros_like(total)
    for c in copies:
        c.wait()

    @pl.loop(0, count)
    def _(g):
        pltpu.make_async_copy(panels[0], held.at[g], sems.at[g]).wait()
        part, first = part_ref[g], first_ref[g]
        for r in range(per):
            at = place_ref[first + r]
            column = pl.ds(pl.multiple_of(lax.rem(at, wide) * TILE, TILE), TILE)
            found = jnp.dot(
                left_ref[at // wide, :, column],
                held[g, r * TILE : (r + 1) * TILE, :],
                preferred_element_type=jnp.float32,
            )
            for j in range(width // TILE):
                for b in range(rows // PBLK):
                    mark = screen_ref[(b * tiles + first + r) * across + part * (width // TILE) + j]
                    strip = slice(b * PBLK, (b + 1) * PBLK)
                    total[part, j, strip, :] += mark * found[strip, j * TILE : (j + 1) * TILE]

    chunks, piece, _ = out_ref.shape
    for i in range(total.shape[0] * total.shape[1]):
        for c in range(chunks):
            strip = total[i // 2, i % 2, c * piece : (c + 1) * piece, :]
            out_ref[c, :, i * TILE : (i + 1) * TILE] = strip.astype(out_ref.dtype)


def ladder(where, place, screen, blocks, panels):
    depth, width = panels[0].shape
    rows = blocks[0].shape[1]
    count, pieces = len(panels), sum(b.shape[0] for b in blocks)
    chunks = NX * NY
    return pl.pallas_call(
        functools.partial(ladder_kernel, count),
        out_shape=jax.ShapeDtypeStruct((chunks, rows // chunks, ZL * width), jnp.bfloat16),
        in_specs=[SMEM] * 4 + [HBM] * (len(blocks) + count),
        out_specs=VMEM,
        scratch_shapes=[
            pltpu.VMEM((pieces,) + blocks[0].shape[1:], jnp.bfloat16),
            pltpu.VMEM((count, depth, width), jnp.bfloat16),
            pltpu.VMEM((ZL, width // TILE, rows, TILE), jnp.float32),
            pltpu.SemaphoreType.DMA((len(blocks),)),
            pltpu.SemaphoreType.DMA((count,)),
        ],
        compiler_params=pltpu.CompilerParams(vmem_limit_bytes=40 << 20),
        cost_estimate=pl.CostEstimate(
            flops=2 * rows * width * count * depth,
            bytes_accessed=(rows + width) * count * depth * 2,
            transcendentals=0,
        ),
        name="ladder",
    )(*where, place, screen, *blocks, *panels)


def reorder_kernel(owner_ref, src_ref, dst_ref):
    for s in range(owner_ref.shape[0]):
        t = owner_ref[s]
        tile = src_ref[t // 4, :, pl.ds(pl.multiple_of(lax.rem(t, 4) * TILE, TILE), TILE)]
        device, j = s // 2, s % 2
        target = device % ZL * NX * NY + device // ZL
        dst_ref[target, :, j * TILE : (j + 1) * TILE] = tile


def reorder(owner, spread):
    n, rows, width = spread.shape
    return pl.pallas_call(
        reorder_kernel,
        out_shape=jax.ShapeDtypeStruct((n * ZL, rows, width // ZL), spread.dtype),
        in_specs=[SMEM, VMEM],
        out_specs=VMEM,
        compiler_params=pltpu.CompilerParams(vmem_limit_bytes=8 << 20),
        cost_estimate=pl.CostEstimate(flops=0, bytes_accessed=1 << 20, transcendentals=0),
        name="reorder",
    )(owner, spread)


def local(amplitudes, tile_owner, integrals, screening, occ_energy, virt_energy):
    pairs, width = amplitudes.shape
    half = pairs // ZL
    tiles = tile_owner.shape[0]
    zh, core, x, y, zl = (lax.axis_index(a) for a in AXES)
    line = x * NY + y
    steps = jnp.arange(tiles, dtype=jnp.int32)

    other = lax.dynamic_slice_in_dim(amplitudes, (1 - zl) * half, half, 0)
    other = send(other, lambda zh, core, x, y, zl: (zh, core, x, y, 1 - zl))
    mine = lax.dynamic_slice_in_dim(amplitudes, zl * half, half, 0)
    blocks, panels = gather(jnp.concatenate([mine, other], axis=1), integrals)

    far, close = (jnp.array(v, jnp.int32) for v in zip(*amplitude_steps()))
    dx, dy = jnp.where(core == 0, close, far), jnp.where(core == 0, far, close)
    device = (((x + dx) % NX) * NY + (y + dy) % NY)[:, None] * ZL + (zl ^ jnp.arange(ZL, dtype=jnp.int32))
    slots = (2 * device[:, :, None] + jnp.arange(2, dtype=jnp.int32)).reshape(-1)
    held = jnp.sum(jnp.where(slots[:, None] == steps[None, :], tile_owner[None, :], 0), axis=1)
    place = jnp.sum(jnp.where(held[:, None] == steps[None, :], steps[:, None], 0), axis=0)

    across = ZL * width // TILE
    screen = lax.dynamic_slice(
        screening, (zl * (half // PBLK), 0, line * across), (half // PBLK, tiles, across)
    )
    screen = screen.astype(jnp.float32).reshape(-1)
    step, flip = (jnp.array(v, jnp.int32) for v in zip(*panel_steps()))
    chip = (zh * ZL + zl + step * (2 * core - 1)) % (ZH * ZL)
    first = (chip // ZL * CORE + (core ^ flip)) * (integrals.shape[0] // TILE)
    where = (first.astype(jnp.int32), (chip % ZL).astype(jnp.int32))
    found = ladder(where, place, screen, blocks, panels)
    spread = lax.all_to_all(found, ("x", "y"), 0, 0, tiled=True)
    sent = reorder(tile_owner, spread)
    total = lax.all_to_all(sent, ("zl", "x", "y"), 0, 0, tiled=True)
    total = total.reshape(pairs, width).astype(jnp.float32)

    own = 2 * (line * ZL + zl)
    virt_owned = jnp.concatenate(
        [lax.dynamic_slice_in_dim(virt_energy, tile_owner[own + i] * TILE, TILE, 0) for i in range(2)]
    )
    residual = total + (virt_owned[None, :] - occ_energy[:, None]) * amplitudes.astype(jnp.float32)
    return residual.astype(jnp.bfloat16)


def solution(mesh):
    fine = Mesh(mesh.devices.reshape(ZH, CORE, NX, NY, ZL), AXES)
    pair, vcol = ("zh", "core"), ("x", "y", "zl")
    return jax.shard_map(
        local,
        mesh=fine,
        in_specs=(P(pair, vcol), P(), P(pair, vcol), P(pair, None, None), P(pair), P()),
        out_specs=P(pair, vcol),
        check_vma=False,
    )
```
